128 devices in a mesh: tm: 16 (over y_hi, x, core), height: 8 (over y_lo, z).
Axes of the slice: x: 4, y: 4 (y_hi: 2, y_lo: 2; y = y_hi * 2 + y_lo), z: 4, core: 2. Of those that a mesh axis runs over, the one named last changes fastest.
Arguments:
- hidden: bfloat16 [32, 16, 128, 1536], P('tm', 'height'), may hold values from -6 to 6
- control: bfloat16 [32, 16, 8192], P('tm', 'height'), may hold values from -6 to 6
- conv_weight: bfloat16 [1728, 256], replicated, may hold values from -0.15625 to 0.15625
- ctrl_proj: bfloat16 [256, 1536], replicated, may hold values from -0.375 to 0.375
- mod_gain: float32 [1536], replicated, may hold values from 0.1 to 1.9
- mod_shift: float32 [1536], replicated, may hold values from -3 to 3
- w_qkv: bfloat16 [1536, 4608], replicated, may hold values from -0.15625 to 0.15625
- kv_stale: bfloat16 [32, 16, 128, 3072], P('tm', 'height'), may hold values from -64 to 64
- key_tiles: int32 [16, 8, 4, 8], P('tm', 'height'), may hold values from 0 to 511, as said below
- key_count: int32 [16, 8, 4], P('tm', 'height'), may hold values from 1 to 8, as said below
Outputs:
- attended: bfloat16 [32, 16, 128, 1536], P('tm', 'height')
- fresh_kv: bfloat16 [32, 16, 128, 3072], P('tm', 'height')
The draws below stay inside these ranges and needn't reach their ends.
Inputs may be any that keep to these rules, and one draw needn't show every extreme that they name: `key_tiles`: with tile t = (a 8 + b) * 4 + c, the entries of list (a, b, c) are distinct tiles other than t itself, each with the same a and b differing by at most 1, or the same b and a differing by 1, 2 or 4. Only the first key_count entries are read. `key_count`: some list uses all 8 entries and some list only one.
All inputs are finite; a program needn't handle non-finite values.
Results may differ from the reference program's by a relative error of at most 0.012.
Values may be sent and summed in bfloat16 or wider, within the bound.
No kernel may reach another device: no remote copies, remote signals or barrier semaphores. Data moves between devices by JAX's collectives and lax.ppermute only.
A program may use at most 448 MiB of HBM per device.

```python
import jax
import jax.numpy as jnp
from jax import lax

D = 1536
HEADS = 12
HD = 128
CIN = 64
CH = 256
FT = 2
HR = 2
TW = 32
TPD = 4
LIST = 8
HA = 1536
W = 128
NF = 32
NH = 16
TA = 16
TB = 8
TT = 128
NTILE = 512


FRAME_STEPS = (0, 0, 0, -1, 1, -2, 2, -4, 4)


ROW_STEPS = (0, -1, 1, 0, 0, 0, 0, 0, 0)


def draw_kv_stale(key, part):
    key = jax.random.fold_in(key, 37)
    first = jax.random.fold_in(key, 0)
    shape = (NF, NH, W, 2 * HA)
    result = jax.random.truncated_normal(first, -4.0, 4.0, shape, jnp.float32)
    return result.astype(jnp.bfloat16)


def draw_key_tiles(key, part):
    key = jax.random.fold_in(key, 23)
    ncand = 9 * TPD
    index = jnp.arange(ncand, dtype=jnp.int32)
    source = index // TPD
    column = index % TPD
    frame_off = jnp.array(FRAME_STEPS, jnp.int32)[source]
    row_off = jnp.array(ROW_STEPS, jnp.int32)[source]
    frame_at = jnp.arange(TA, dtype=jnp.int32)[:, None, None, None] + frame_off
    row_at = jnp.arange(TB, dtype=jnp.int32)[None, :, None, None] + row_off
    own_col = jnp.arange(TPD, dtype=jnp.int32)[None, None, :, None]
    valid = (frame_at >= 0) & (frame_at < TA) & (row_at >= 0) & (row_at < TB)
    valid = valid & jnp.logical_not((source == 0) & (column == own_col))
    ident = (frame_at * TB + row_at) * TPD + column
    ident = jnp.broadcast_to(ident, (TA, TB, TPD, ncand))
    draws = jax.random.randint(key, (TA, TB, TPD, ncand), 0, 1 << 20)
    score = jnp.where(valid, draws * ncand + index, -1)
    picked = lax.top_k(score, LIST)[1]
    return jnp.take_along_axis(ident, picked, axis=-1).astype(jnp.int32)


def draw_key_count(key, part):
    key = jax.random.fold_in(key, 11)
    first, second = jax.random.split(key)
    left = jax.random.randint(first, (TA, TB, TPD), 0, LIST)
    right = jax.random.randint(second, (TA, TB, TPD), 0, LIST + 1)
    count = LIST - left * right // 16
    count = jnp.clip(count, 1, LIST)
    count = count.at[0, 0, 0].set(LIST)
    count = count.at[TA - 1, TB - 1, TPD - 1].set(1)
    return count.astype(jnp.int32)


def block_scale(stream_key, extent, shards, low, top_value):
    loudness, own = 1.0, jax.random.fold_in(stream_key, 6)
    for dim, blocks in shards:
        steps = jnp.exp(jax.random.uniform(jax.random.fold_in(own, dim), (blocks,), jnp.float32, low / len(shards), top_value / len(shards)))
        loudness = loudness * jnp.repeat(steps, extent[dim] // blocks).reshape([-1 if axis == dim else 1 for axis in range(len(extent))])
    return loudness


def scatter_about(stream_key, shape, width, limit, pieces=(), kind=jnp.bfloat16):
    factor_of = block_scale(stream_key, shape, pieces, -0.22, 0.18) if pieces else 1.0
    values = jax.random.normal(stream_key, shape, jnp.float32) * width * factor_of
    return jnp.minimum(jnp.maximum(values, -limit), limit).astype(kind)


def setup_inputs(seed: int = 0) -> dict:
    splits = jax.random.split(jax.random.key(seed), 11)
    return {
        "hidden": scatter_about(splits[0], (NF, NH, W, D), 1.0, 6.0, ((0, 16), (1, 8))),
        "control": scatter_about(splits[1], (NF, NH, W * CIN), 1.0, 6.0, ((0, 16), (1, 8))),
        "conv_weight": scatter_about(splits[2], (27 * CIN, CH), (27 * CIN) ** -0.5, 0.15625),
        "ctrl_proj": scatter_about(splits[3], (CH, D), CH ** -0.5, 0.375),
        "mod_gain": jnp.clip(1.0 + 0.18 * jax.random.normal(splits[4], (D,), jnp.float32), 0.1, 1.9),
        "mod_shift": scatter_about(splits[5], (D,), 0.5, 3.0, (), jnp.float32),
        "w_qkv": scatter_about(splits[6], (D, 3 * HA), D ** -0.5, 0.15625),
        "kv_stale": draw_kv_stale(jax.random.fold_in(splits[10], 71), 0),
        "key_tiles": draw_key_tiles(jax.random.fold_in(splits[10], 71), 0),
        "key_count": draw_key_count(jax.random.fold_in(splits[10], 71), 0),
    }


def to_tiles(grid):
    chan = grid.shape[-1]
    blocks = grid.reshape(TA, FT, TB, HR, TPD, TW, chan)
    return blocks.transpose(0, 2, 4, 1, 3, 5, 6).reshape(NTILE, TT, chan)

def from_tiles(tiles):
    chan = tiles.shape[-1]
    blocks = tiles.reshape(TA, TB, TPD, FT, HR, TW, chan)
    return blocks.transpose(0, 3, 1, 4, 2, 5, 6).reshape(NF, NH, W, chan)

def reference(hidden, control, conv_weight, ctrl_proj, mod_gain, mod_shift, w_qkv, kv_stale, key_tiles, key_count):
    grid = control.reshape(NF, NH, W, CIN)
    padded = jnp.pad(grid, ((1, 1), (1, 1), (1, 1), (0, 0)))
    taps = [padded[i:i + NF, j:j + NH, k:k + W] for i in range(3) for j in range(3) for k in range(3)]
    stacked = jnp.concatenate(taps, axis=-1).reshape(NF * NH * W, 27 * CIN)
    conv = jnp.dot(stacked, conv_weight, preferred_element_type=jnp.float32)
    act = jax.nn.silu(conv).astype(jnp.bfloat16)
    mixed = hidden.reshape(NF * NH * W, D).astype(jnp.float32) + jnp.dot(act, ctrl_proj, preferred_element_type=jnp.float32)
    center = mixed - lax.optimization_barrier(jnp.mean(mixed, axis=-1, keepdims=True))
    spread = lax.optimization_barrier(jnp.mean(center * center, axis=-1, keepdims=True))
    normed = (center * lax.rsqrt(spread + 1e-06) * mod_gain + mod_shift).astype(jnp.bfloat16)
    qkv = jnp.dot(normed, w_qkv, preferred_element_type=jnp.float32).astype(jnp.bfloat16)
    qkv_grid = qkv.reshape(NF, NH, W, 3 * HA)
    fresh_kv = qkv_grid[..., HA:]
    query_tiles = to_tiles(qkv_grid[..., :HA])
    fresh_tiles = to_tiles(fresh_kv)
    stale_tiles = to_tiles(kv_stale)
    lists = key_tiles.reshape(NTILE, LIST)
    counts = key_count.reshape(NTILE)
    scale = HD ** (-0.5)

    def one_tile(item):
        query, fresh, listed, count = item
        far = stale_tiles[listed].reshape(LIST * TT, 2 * HA)
        keyval = jnp.concatenate([fresh, far], axis=0).astype(jnp.float32)
        keys = keyval[:, :HA].reshape(-1, HEADS, HD)
        values = keyval[:, HA:].reshape(-1, HEADS, HD)
        heads_q = query.astype(jnp.float32).reshape(TT, HEADS, HD)
        scores = jnp.einsum('qhd,khd->hqk', heads_q, keys) * scale
        slot = jnp.arange(TT * (LIST + 1)) // TT
        live = slot <= count
        scores = jnp.where(live[None, None, :], scores, -jnp.inf)
        top = lax.optimization_barrier(jnp.max(scores, axis=-1, keepdims=True))
        probs = jnp.exp(scores - top)
        total = lax.optimization_barrier(jnp.sum(probs, axis=-1))
        weights = lax.optimization_barrier(probs.astype(jnp.bfloat16)).astype(jnp.float32)
        summed = jnp.einsum('hqk,khd->qhd', weights, values)
        result = summed / total.T[:, :, None]
        return result.reshape(TT, HA).astype(jnp.bfloat16)
    attended_tiles = lax.map(one_tile, (query_tiles, fresh_tiles, lists, counts))
    return (from_tiles(attended_tiles), fresh_kv)
```

```python
import functools

import jax
import jax.numpy as jnp
from jax import lax
from jax.experimental import pallas as pl
from jax.experimental.pallas import tpu as pltpu
from jax.sharding import PartitionSpec as P

HEADS = 12
HD = 128
LOG2E = 1.4426950408889634


FRAME_STEPS = (0, 0, 0, -1, 1, -2, 2, -4, 4)
ROW_STEPS = (0, -1, 1, 0, 0, 0, 0, 0, 0)
GROUPS = ((0, 1, 2), (3, 4, 5, 6), (7, 8))


def with_halo(cells, sides, width):
    for axis, dim in sides:
        count = lax.axis_size(axis)
        ends = count - 1
        head = lax.slice_in_dim(cells, 0, width, axis=dim)
        tail = lax.slice_in_dim(cells, cells.shape[dim] - width, cells.shape[dim], axis=dim)
        cells = jnp.concatenate(
            [
                lax.ppermute(tail, axis, [(i, (i + 1) % count) for i in range(ends)]),
                cells,
                lax.ppermute(head, axis, [((i + 1) % count, i) for i in range(ends)]),
            ],
            axis=dim,
        )
    return cells


def from_behind(block, axis, distance):
    devices = range(lax.axis_size(axis))
    route = [(i - distance, i) for i in devices if i - distance in devices]
    return lax.ppermute(block, axis, route)


def attend_kernel(ids, first, last, *refs):
    code_ref, q_ref = refs[0], refs[1]
    stale = refs[2 : 2 + len(ids)]
    rest = refs[2 + len(ids) :]
    if not first:
        acc_in, top_in, sum_in = rest[:3]
        rest = rest[3:]
    if last:
        out_ref, acc, top, total = rest
    else:
        acc, top, total = rest
    planes, cols = q_ref.shape[0], q_ref.shape[1]
    tokens = planes * cols
    width = HEADS * HD
    tile = pl.program_id(0)
    scale = HD**-0.5 * LOG2E
    ones = jnp.ones((tokens, HD), jnp.bfloat16)

    def parts(head, key, value):
        query = q_ref[:, :, head * HD : (head + 1) * HD].reshape(tokens, HD)
        s = lax.dot_general(
            query, key, (((1,), (1,)), ((), ())), preferred_element_type=jnp.float32
        )
        return s * scale, jnp.concatenate([value, ones], axis=1)

    if first:
        for head in range(HEADS):
            low = width + head * HD
            key = q_ref[:, :, low : low + HD].reshape(tokens, HD)
            value = q_ref[:, :, low + width : low + width + HD].reshape(tokens, HD)
            s, both = parts(head, key, value)
            new = jnp.max(s, axis=1, keepdims=True)
            p = jnp.exp2(s - new).astype(jnp.bfloat16)
            got = jnp.dot(p, both, preferred_element_type=jnp.float32)
            acc[0, head] = got[:, :HD]
            total[0, head] = got[:, HD:]
            top[0, head] = jnp.broadcast_to(new, (tokens, HD))
    else:
        acc[...] = acc_in[...]
        top[...] = top_in[...]
        total[...] = sum_in[...]

    def slot(place, carry):
        code = code_ref[tile * 8 + place]
        for which, kv_ref in zip(ids, stale):

            @pl.when(code >> 2 == which)
            def _():
                here = pl.ds(pl.multiple_of((code & 3) * cols, cols), cols)
                for head in range(HEADS):
                    low = head * HD
                    key = kv_ref[:, here, low : low + HD].reshape(tokens, HD)
                    value = kv_ref[:, here, width + low : width + low + HD].reshape(tokens, HD)
                    s, both = parts(head, key, value)
                    old = top[0, head]
                    new = jnp.maximum(old, jnp.max(s, axis=1, keepdims=True))
                    alpha = jnp.exp2(old - new)
                    p = jnp.exp2(s - new).astype(jnp.bfloat16)
                    got = jnp.dot(p, both, preferred_element_type=jnp.float32)
                    acc[0, head] = acc[0, head] * alpha + got[:, :HD]
                    total[0, head] = total[0, head] * alpha + got[:, HD:]
                    top[0, head] = new

        return carry

    lax.fori_loop(0, 8, slot, 0)
    if last:
        for head in range(HEADS):
            res = (acc[0, head] / total[0, head]).astype(jnp.bfloat16)
            out_ref[:, :, head * HD : (head + 1) * HD] = res.reshape(planes, cols, HD)


def attend(code, qkv, sources, state, last):
    ids = tuple(which for which, _ in sources)
    planes, width, full = qkv.shape
    tiles = code.shape[0] // 8
    cols = width // tiles
    tokens = planes * cols
    first = state is None
    keep = pl.BlockSpec((1, HEADS, tokens, HD), lambda t: (t, 0, 0, 0))
    whole = pl.BlockSpec(
        (planes, width, 2 * HEADS * HD), lambda t: (0, 0, 0), pipeline_mode=pl.Buffered(1)
    )
    part = (planes, cols, HEADS * HD)
    qpart = (planes, cols, full) if first else part
    in_specs = [pl.BlockSpec(memory_space=pltpu.SMEM), pl.BlockSpec(qpart, lambda t: (0, t, 0))]
    in_specs += [whole] * len(ids)
    operands = [code, qkv] + [block for _, block in sources]
    if not first:
        in_specs += [keep] * 3
        operands += list(state)
    kept = jax.ShapeDtypeStruct((tiles, HEADS, tokens, HD), jnp.float32)
    if last:
        out_shape = jax.ShapeDtypeStruct((planes, width, HEADS * HD), jnp.bfloat16)
        out_specs = pl.BlockSpec(part, lambda t: (0, t, 0))
        scratch = [pltpu.VMEM((1, HEADS, tokens, HD), jnp.float32)] * 3
    else:
        out_shape = [kept] * 3
        out_specs = [keep] * 3
        scratch = []
    return pl.pallas_call(
        functools.partial(attend_kernel, ids, first, last),
        grid=(tiles,),
        in_specs=in_specs,
        out_specs=out_specs,
        out_shape=out_shape,
        scratch_shapes=scratch,
        compiler_params=pltpu.CompilerParams(vmem_limit_bytes=56 << 20),
        cost_estimate=pl.CostEstimate(
            flops=1_000_000_000, bytes_accessed=40_000_000, transcendentals=3_000_000
        ),
    )(*operands)


def body(
    hidden,
    control,
    conv_weight,
    ctrl_proj,
    mod_gain,
    mod_shift,
    w_qkv,
    kv_stale,
    key_tiles,
    key_count,
):
    frames, rows, width, dmodel = hidden.shape
    tiles_dev = key_count.shape[2]
    cin = conv_weight.shape[0] // 27
    attn_width = HEADS * HD
    planes = frames * rows
    rim = with_halo(control, (("tm", 0), ("height", 1)), 1)
    grid = rim.reshape(frames + 2, rows + 2, width, cin)
    grid = jnp.pad(grid, ((0, 0), (0, 0), (1, 1), (0, 0)))
    taps = [
        grid[i : i + frames, j : j + rows, k : k + width]
        for i in range(3)
        for j in range(3)
        for k in range(3)
    ]
    stacked = jnp.concatenate(taps, axis=-1).reshape(frames * rows * width, 27 * cin)
    conv = jnp.dot(stacked, conv_weight, preferred_element_type=jnp.float32)
    act = jax.nn.silu(conv).astype(jnp.bfloat16)
    mixed = hidden.reshape(frames * rows * width, dmodel).astype(jnp.float32) + jnp.dot(
        act, ctrl_proj, preferred_element_type=jnp.float32
    )
    center = mixed - jnp.mean(mixed, axis=-1, keepdims=True)
    spread = jnp.mean(center * center, axis=-1, keepdims=True)
    normed = (center * lax.rsqrt(spread + 1e-06) * mod_gain + mod_shift).astype(jnp.bfloat16)
    qkv = jnp.dot(normed, w_qkv, preferred_element_type=jnp.float32).astype(jnp.bfloat16)
    qkv_grid = qkv.reshape(frames, rows, width, 3 * attn_width)
    fresh_kv = qkv_grid[..., attn_width:]
    blocks = {0: kv_stale}
    tm_axis, h_axis = "tm", "height"
    for which in range(1, 3):
        blocks[which] = from_behind(kv_stale, h_axis, -ROW_STEPS[which])
    for which in range(3, 9):
        blocks[which] = from_behind(kv_stale, tm_axis, -FRAME_STEPS[which])
    frame_idx = lax.axis_index("tm")
    row_idx = lax.axis_index("height")
    row_total = lax.axis_size("height")
    idents = key_tiles[0, 0]
    counts = key_count[0, 0]
    dframe = idents // (row_total * tiles_dev) - frame_idx
    drow = idents // tiles_dev % row_total - row_idx
    source = jnp.zeros_like(idents)
    for which in range(9):
        hit = (dframe == FRAME_STEPS[which]) & (drow == ROW_STEPS[which])
        source = source + which * hit.astype(jnp.int32)
    used = lax.broadcasted_iota(jnp.int32, idents.shape, 1) < counts[:, None]
    code = jnp.where(used, source * 4 + idents % tiles_dev, -1).reshape(-1)
    qkv = qkv.reshape(planes, width, 3 * attn_width)
    flat = {w: x.reshape(planes, width, 2 * attn_width) for w, x in blocks.items()}
    state = None
    for group in GROUPS:
        state = attend(code, qkv, [(w, flat[w]) for w in group], state, group is GROUPS[-1])
    return (state.reshape(frames, rows, width, attn_width), fresh_kv)


def solution(mesh):
    placed = (
        P("tm", "height", None, None),
        P("tm", "height", None),
        P(),
        P(),
        P(),
        P(),
        P(),
        P("tm", "height", None, None),
        P("tm", "height", None, None),
        P("tm", "height", None),
    )
    return jax.shard_map(
        body,
        mesh=mesh,
        in_specs=placed,
        out_specs=(P("tm", "height", None, None), P("tm", "height", None, None)),
        check_vma=False,
    )
```

```python
import functools

import jax
import jax.numpy as jnp
from jax import lax
from jax.experimental import pallas as pl
from jax.experimental.pallas import tpu as pltpu
from jax.sharding import PartitionSpec as P

HEADS = 12
HD = 128
LOG2E = 1.4426950408889634
AHEAD = 2
RING = 8
GROUPS = ((0, 3), (1, 2, 4, 5, 6, 7), (8,), (9, 10, 11, 12), (13,))
COSTS = (30, 50, 20, 8, 8)


def around(device, step):
    return device // RING * RING + (device + step) % RING


def swap(parity):
    return [(i, i ^ 1) for i in range(2 * RING) if i % 2 == parity]


def fetch_blocks(kv):
    everyone = range(2 * RING)
    half = kv.shape[-1] // 2
    up = [(i, around(i, 2)) for i in everyone]
    down = [(i, around(i, -2)) for i in everyone]
    over = [(0, 8), (1, 9), (2, 10), (3, 11), (12, 4), (13, 5), (14, 6), (15, 7)]
    below = lax.ppermute(kv, "tm", up)
    above = lax.ppermute(kv, "tm", down)
    rows_before = from_behind(kv, "height", 1)
    rows_after = from_behind(kv, "height", -1)
    mate = lax.ppermute(kv, "tm", swap(0) + swap(1))
    odd_below = lax.ppermute(below, "tm", swap(1))
    even_above = lax.ppermute(above, "tm", swap(0))
    far_keys = lax.ppermute(below[..., :half], "tm", up)
    far_values = lax.ppermute(above[..., half:], "tm", down)
    across_below = lax.ppermute(below, "tm", [(0, 8), (1, 9)])
    across_above = lax.ppermute(above, "tm", [(14, 6), (15, 7)])
    mate_below = lax.ppermute(across_below, "tm", [(9, 8)])
    mate_above = lax.ppermute(across_above, "tm", [(6, 7)])
    across_keys = lax.ppermute(far_keys, "tm", over)
    across_values = lax.ppermute(far_values, "tm", over)
    singles = (kv, rows_before, rows_after, mate, below, above, odd_below, even_above)
    crossed = (across_below, across_above, mate_below, mate_above)
    halves = [(block,) for block in singles] + [(far_keys, far_values)]
    return halves + [(block,) for block in crossed] + [(across_keys, across_values)]


def locate(dframe, drow, frame_idx):
    odd = frame_idx % 2
    spot = frame_idx % RING // 2
    low, high, left = spot == 0, spot == RING // 2 - 1, spot < 2
    table = {
        -1: jnp.where(odd == 1, 3, jnp.where(low, 11, 6)),
        1: jnp.where(odd == 0, 3, jnp.where(high, 12, 7)),
        -2: jnp.where(low, 9, 4),
        2: jnp.where(high, 10, 5),
        -4: jnp.where(left, 13, 8),
        4: jnp.where(left, 8, 13),
    }
    source = jnp.where(drow == -1, 1, jnp.where(drow == 1, 2, 0))
    for step, place in table.items():
        source = jnp.where(dframe == step, place, source)
    return source


def with_halo(cells, sides, width):
    for axis, dim in sides:
        count = lax.axis_size(axis)
        ends = count - 1
        head = lax.slice_in_dim(cells, 0, width, axis=dim)
        tail = lax.slice_in_dim(cells, cells.shape[dim] - width, cells.shape[dim], axis=dim)
        cells = jnp.concatenate(
            [
                lax.ppermute(tail, axis, [(i, (i + 1) % count) for i in range(ends)]),
                cells,
                lax.ppermute(head, axis, [((i + 1) % count, i) for i in range(ends)]),
            ],
            axis=dim,
        )
    return cells


def from_behind(block, axis, distance):
    devices = range(lax.axis_size(axis))
    route = [(i - distance, i) for i in devices if i - distance in devices]
    return lax.ppermute(block, axis, route)


def attend_kernel(ids, first, last, *refs):
    code_ref, q_ref = refs[0], refs[1]
    count = sum(n for _, n in ids)
    rest = refs[2 + count :]
    stale = []
    at = 2
    for which, n in ids:
        stale.append((which, refs[at], refs[at + n - 1], n == 1))
        at += n
    if not first:
        acc_in, top_in, sum_in = rest[:3]
        rest = rest[3:]
    if last:
        out_ref, acc, top, total = rest
    else:
        acc, top, total = rest
    planes, cols = q_ref.shape[0], q_ref.shape[1]
    tokens = planes * cols
    width = HEADS * HD
    tile = pl.program_id(0)
    scale = HD**-0.5 * LOG2E

    def add_tile(key_of, value_of, fresh):
        def scores(head):
            query = q_ref[:, :, head * HD : (head + 1) * HD].reshape(tokens, HD)
            return lax.dot_general(
                key_of(head), query, (((1,), (1,)), ((), ())), preferred_element_type=jnp.float32
            )

        ready = [scores(head) for head in range(AHEAD)]
        for head in range(HEADS):
            if head + AHEAD < HEADS:
                ready.append(scores(head + AHEAD))
            s = ready[head]
            new = jnp.max(s, axis=0, keepdims=True)
            if not fresh:
                old = top[0, head : head + 1]
                new = jnp.maximum(old, new)
                alpha = jnp.exp2((old - new) * scale)
            p = jnp.exp2((s - new) * scale)
            gain = jnp.sum(p, axis=0, keepdims=True)
            got = lax.dot_general(
                value_of(head),
                p.astype(jnp.bfloat16),
                (((0,), (0,)), ((), ())),
                preferred_element_type=jnp.float32,
            )
            if not fresh:
                gain = total[0, head : head + 1] * alpha + gain
                got = acc[0, head] * alpha + got
            top[0, head : head + 1] = new
            total[0, head : head + 1] = gain
            acc[0, head] = got

    if first:

        def fresh_part(low):
            return q_ref[:, :, low : low + HD].reshape(tokens, HD)

        add_tile(
            lambda head: fresh_part(width + head * HD),
            lambda head: fresh_part(2 * width + head * HD),
            True,
        )
    else:
        acc[...] = acc_in[...]
        top[...] = top_in[...]
        total[...] = sum_in[...]

    def slot(place, carry):
        code = code_ref[tile * 8 + place]
        for which, key_ref, value_ref, joined in stale:

            @pl.when(code >> 2 == which)
            def _():
                here = pl.ds(pl.multiple_of((code & 3) * cols, cols), cols)
                shift = width if joined else 0

                def key_of(head):
                    low = head * HD
                    return key_ref[:, here, low : low + HD].reshape(tokens, HD)

                def value_of(head):
                    low = shift + head * HD
                    return value_ref[:, here, low : low + HD].reshape(tokens, HD)

                add_tile(key_of, value_of, False)

        return carry

    lax.fori_loop(0, 8, slot, 0)
    if last:
        for head in range(HEADS):
            res = acc[0, head] / total[0, head : head + 1]
            res = jnp.transpose(res).astype(jnp.bfloat16)
            out_ref[:, :, head * HD : (head + 1) * HD] = res.reshape(planes, cols, HD)


def attend(code, qkv, sources, state, last, cost):
    ids = tuple((which, len(blocks)) for which, blocks in sources)
    blocks = [block for _, parts in sources for block in parts]
    planes, width, full = qkv.shape
    tiles = code.shape[0] // 8
    cols = width // tiles
    tokens = planes * cols
    first = state is None
    keep = pl.BlockSpec((1, HEADS, HD, tokens), lambda t: (t, 0, 0, 0))
    keep_row = pl.BlockSpec((1, HEADS, tokens), lambda t: (t, 0, 0))

    def whole(block):
        once = pl.Buffered(1)
        return pl.BlockSpec(block.shape, lambda t: (0, 0, 0), pipeline_mode=once)

    part = (planes, cols, HEADS * HD)
    qpart = (planes, cols, full) if first else part
    in_specs = [pl.BlockSpec(memory_space=pltpu.SMEM), pl.BlockSpec(qpart, lambda t: (0, t, 0))]
    in_specs += [whole(block) for block in blocks]
    operands = [code, qkv] + blocks
    if not first:
        in_specs += [keep, keep_row, keep_row]
        operands += list(state)
    kept = jax.ShapeDtypeStruct((tiles, HEADS, HD, tokens), jnp.float32)
    kept_row = jax.ShapeDtypeStruct((tiles, HEADS, tokens), jnp.float32)
    if last:
        out_shape = jax.ShapeDtypeStruct((planes, width, HEADS * HD), jnp.bfloat16)
        out_specs = pl.BlockSpec(part, lambda t: (0, t, 0))
        scratch = [pltpu.VMEM((1, HEADS, HD, tokens), jnp.float32)]
        scratch += [pltpu.VMEM((1, HEADS, tokens), jnp.float32)] * 2
    else:
        out_shape = [kept, kept_row, kept_row]
        out_specs = [keep, keep_row, keep_row]
        scratch = []
    return pl.pallas_call(
        functools.partial(attend_kernel, ids, first, last),
        grid=(tiles,),
        in_specs=in_specs,
        out_specs=out_specs,
        out_shape=out_shape,
        scratch_shapes=scratch,
        compiler_params=pltpu.CompilerParams(vmem_limit_bytes=56 << 20),
        cost_estimate=pl.CostEstimate(
            flops=cost * 1_000_000_000, bytes_accessed=cost * 3_000_000, transcendentals=0
        ),
    )(*operands)


def body(
    hidden,
    control,
    conv_weight,
    ctrl_proj,
    mod_gain,
    mod_shift,
    w_qkv,
    kv_stale,
    key_tiles,
    key_count,
):
    frames, rows, width, dmodel = hidden.shape
    tiles_dev = key_count.shape[2]
    cin = conv_weight.shape[0] // 27
    attn_width = HEADS * HD
    planes = frames * rows
    rim = with_halo(control, (("tm", 0), ("height", 1)), 1)
    rim, kv_stale = lax.optimization_barrier((rim, kv_stale))
    grid = rim.reshape(frames + 2, rows + 2, width, cin)
    grid = jnp.pad(grid, ((0, 0), (0, 0), (1, 1), (0, 0)))
    taps = [
        grid[i : i + frames, j : j + rows, k : k + width]
        for i in range(3)
        for j in range(3)
        for k in range(3)
    ]
    stacked = jnp.concatenate(taps, axis=-1).reshape(frames * rows * width, 27 * cin)
    conv = jnp.dot(stacked, conv_weight, preferred_element_type=jnp.float32)
    act = jax.nn.silu(conv).astype(jnp.bfloat16)
    mixed = hidden.reshape(frames * rows * width, dmodel).astype(jnp.float32) + jnp.dot(
        act, ctrl_proj, preferred_element_type=jnp.float32
    )
    center = mixed - jnp.mean(mixed, axis=-1, keepdims=True)
    spread = jnp.mean(center * center, axis=-1, keepdims=True)
    normed = (center * lax.rsqrt(spread + 1e-06) * mod_gain + mod_shift).astype(jnp.bfloat16)
    qkv = jnp.dot(normed, w_qkv, preferred_element_type=jnp.float32).astype(jnp.bfloat16)
    qkv_grid = qkv.reshape(frames, rows, width, 3 * attn_width)
    fresh_kv = qkv_grid[..., attn_width:]
    frame_idx = lax.axis_index("tm")
    row_idx = lax.axis_index("height")
    row_total = lax.axis_size("height")
    idents = key_tiles[0, 0]
    counts = key_count[0, 0]
    dframe = idents // (row_total * tiles_dev) - frame_idx
    drow = idents // tiles_dev % row_total - row_idx
    source = locate(dframe, drow, frame_idx)
    used = lax.broadcasted_iota(jnp.int32, idents.shape, 1) < counts[:, None]
    code = jnp.where(used, source * 4 + idents % tiles_dev, -1).reshape(-1)
    qkv = qkv.reshape(planes, width, 3 * attn_width)
    blocks = [
        tuple(part.reshape(planes, width, part.shape[-1]) for part in parts)
        for parts in fetch_blocks(kv_stale)
    ]
    state = None
    for group, cost in zip(GROUPS, COSTS):
        state = attend(code, qkv, [(w, blocks[w]) for w in group], state, group is GROUPS[-1], cost)
    return (state.reshape(frames, rows, width, attn_width), fresh_kv)


def solution(mesh):
    placed = (
        P("tm", "height", None, None),
        P("tm", "height", None),
        P(),
        P(),
        P(),
        P(),
        P(),
        P("tm", "height", None, None),
        P("tm", "height", None, None),
        P("tm", "height", None),
    )
    return jax.shard_map(
        body,
        mesh=mesh,
        in_specs=placed,
        out_specs=(P("tm", "height", None, None), P("tm", "height", None, None)),
        check_vma=False,
    )
```

```python
import functools

import jax
import jax.numpy as jnp
from jax import lax
from jax.experimental import pallas as pl
from jax.experimental.pallas import tpu as pltpu
from jax.sharding import PartitionSpec as P

HEADS = 12
HD = 128
LOG2E = 1.4426950408889634
AHEAD = 2
RING = 8


def around(device, step):
    return device // RING * RING + (device + step) % RING


def swap(parity):
    return [(i, i ^ 1) for i in range(2 * RING) if i % 2 == parity]


def nearest(kv):
    everyone = range(2 * RING)
    below = lax.ppermute(kv, "tm", [(i, around(i, 2)) for i in everyone])
    above = lax.ppermute(kv, "tm", [(i, around(i, -2)) for i in everyone])
    rows_before = from_behind(kv, "height", 1)
    rows_after = from_behind(kv, "height", -1)
    mate = lax.ppermute(kv, "tm", swap(0) + swap(1))
    return below, above, rows_before, rows_after, mate


def second(below, above, frame_idx):
    everyone = range(2 * RING)
    half = below.shape[-1] // 2
    from_below = (frame_idx < 2) | (frame_idx == 12) | (frame_idx == 13)
    odd = frame_idx % 2 == 1
    parts = (
        below[..., :half],
        above[..., half:],
        jnp.where(from_below, below[..., :half], above[..., :half]),
        jnp.where(from_below, below[..., half:], above[..., half:]),
    )
    below_keys, above_values, edge_keys, edge_values = lax.optimization_barrier(parts)
    over = [(0, 8), (1, 9), (2, 10), (3, 11), (12, 4), (13, 5), (14, 6), (15, 7)]
    far_keys = lax.ppermute(below_keys, "tm", [(i, around(i, 2)) for i in everyone])
    far_values = lax.ppermute(above_values, "tm", [(i, around(i, -2)) for i in everyone])
    cross_keys = lax.ppermute(edge_keys, "tm", over)
    cross_values = lax.ppermute(edge_values, "tm", over)
    beside = lax.ppermute(jnp.where(odd, below, above), "tm", swap(0) + swap(1))
    return far_keys, far_values, cross_keys, cross_values, beside


def third(cross):
    trade = [(8, 10), (9, 11), (10, 8), (11, 9), (4, 6), (5, 7), (6, 4), (7, 5)]
    return lax.ppermute(cross, "tm", trade), lax.ppermute(cross, "tm", [(9, 8), (6, 7)])


def locate(dframe, drow, frame_idx):
    odd = frame_idx % 2
    spot = frame_idx % RING // 2
    low, high = spot == 0, spot == RING // 2 - 1
    table = {
        -1: jnp.where(odd == 1, 3, jnp.where(low, 9, 6)),
        1: jnp.where(odd == 0, 3, jnp.where(high, 9, 6)),
        -2: jnp.where(low, 8, 4),
        2: jnp.where(high, 8, 5),
        -4: jnp.where(spot < 2, 10, 7),
        4: jnp.where(spot < 2, 7, 10),
    }
    source = jnp.where(drow == -1, 1, jnp.where(drow == 1, 2, 0))
    for step, place in table.items():
        source = jnp.where(dframe == step, place, source)
    return source


def with_halo(cells, sides, width):
    for axis, dim in sides:
        count = lax.axis_size(axis)
        ends = count - 1
        head = lax.slice_in_dim(cells, 0, width, axis=dim)
        tail = lax.slice_in_dim(cells, cells.shape[dim] - width, cells.shape[dim], axis=dim)
        cells = jnp.concatenate(
            [
                lax.ppermute(tail, axis, [(i, (i + 1) % count) for i in range(ends)]),
                cells,
                lax.ppermute(head, axis, [((i + 1) % count, i) for i in range(ends)]),
            ],
            axis=dim,
        )
    return cells


def from_behind(block, axis, distance):
    devices = range(lax.axis_size(axis))
    route = [(i - distance, i) for i in devices if i - distance in devices]
    return lax.ppermute(block, axis, route)


def attend_kernel(ids, first, last, *refs):
    code_ref, q_ref = refs[0], refs[1]
    count = sum(n for _, n in ids)
    rest = refs[2 + count :]
    stale = []
    at = 2
    for which, n in ids:
        stale.append((which, refs[at], refs[at + n - 1], n == 1))
        at += n
    if not first:
        acc_in, top_in, sum_in = rest[:3]
        rest = rest[3:]
    if last:
        out_ref, acc, top, total = rest
    else:
        acc, top, total = rest
    planes, cols = q_ref.shape[0], q_ref.shape[1]
    tokens = planes * cols
    width = HEADS * HD
    tile = pl.program_id(0)
    scale = HD**-0.5 * LOG2E

    def add_tile(key_of, value_of, fresh):
        def scores(head):
            query = q_ref[:, :, head * HD : (head + 1) * HD].reshape(tokens, HD)
            return lax.dot_general(
                key_of(head), query, (((1,), (1,)), ((), ())), preferred_element_type=jnp.float32
            )

        ready = [scores(head) for head in range(AHEAD)]
        for head in range(HEADS):
            if head + AHEAD < HEADS:
                ready.append(scores(head + AHEAD))
            s = ready[head]
            new = jnp.max(s, axis=0, keepdims=True)
            if not fresh:
                old = top[0, head : head + 1]
                new = jnp.maximum(old, new)
                alpha = jnp.exp2((old - new) * scale)
            p = jnp.exp2((s - new) * scale)
            gain = jnp.sum(p, axis=0, keepdims=True)
            got = lax.dot_general(
                value_of(head),
                p.astype(jnp.bfloat16),
                (((0,), (0,)), ((), ())),
                preferred_element_type=jnp.float32,
            )
            if not fresh:
                gain = total[0, head : head + 1] * alpha + gain
                got = acc[0, head] * alpha + got
            top[0, head : head + 1] = new
            total[0, head : head + 1] = gain
            acc[0, head] = got

    if first:

        def fresh_part(low):
            return q_ref[:, :, low : low + HD].reshape(tokens, HD)

        add_tile(
            lambda head: fresh_part(width + head * HD),
            lambda head: fresh_part(2 * width + head * HD),
            True,
        )
    else:
        acc[...] = acc_in[...]
        top[...] = top_in[...]
        total[...] = sum_in[...]

    def slot(place, carry):
        code = code_ref[tile * 8 + place]
        for which, key_ref, value_ref, joined in stale:

            @pl.when(code >> 2 == which)
            def _():
                here = pl.ds(pl.multiple_of((code & 3) * cols, cols), cols)
                shift = width if joined else 0

                def key_of(head):
                    low = head * HD
                    return key_ref[:, here, low : low + HD].reshape(tokens, HD)

                def value_of(head):
                    low = shift + head * HD
                    return value_ref[:, here, low : low + HD].reshape(tokens, HD)

                add_tile(key_of, value_of, False)

        return carry

    lax.fori_loop(0, 8, slot, 0)
    if last:
        for head in range(HEADS):
            res = acc[0, head] / total[0, head : head + 1]
            res = jnp.transpose(res).astype(jnp.bfloat16)
            out_ref[:, :, head * HD : (head + 1) * HD] = res.reshape(planes, cols, HD)


def attend(code, qkv, sources, state, last, cost):
    ids = tuple((which, len(blocks)) for which, blocks in sources)
    blocks = [block for _, parts in sources for block in parts]
    planes, width, full = qkv.shape
    tiles = code.shape[0] // 8
    cols = width // tiles
    tokens = planes * cols
    first = state is None
    keep = pl.BlockSpec((1, HEADS, HD, tokens), lambda t: (t, 0, 0, 0))
    keep_row = pl.BlockSpec((1, HEADS, tokens), lambda t: (t, 0, 0))

    def whole(block):
        once = pl.Buffered(1)
        return pl.BlockSpec(block.shape, lambda t: (0, 0, 0), pipeline_mode=once)

    part = (planes, cols, HEADS * HD)
    qpart = (planes, cols, full) if first else part
    in_specs = [pl.BlockSpec(memory_space=pltpu.SMEM), pl.BlockSpec(qpart, lambda t: (0, t, 0))]
    in_specs += [whole(block) for block in blocks]
    operands = [code, qkv] + blocks
    if not first:
        in_specs += [keep, keep_row, keep_row]
        operands += list(state)
    kept = jax.ShapeDtypeStruct((tiles, HEADS, HD, tokens), jnp.float32)
    kept_row = jax.ShapeDtypeStruct((tiles, HEADS, tokens), jnp.float32)
    if last:
        out_shape = jax.ShapeDtypeStruct((planes, width, HEADS * HD), jnp.bfloat16)
        out_specs = pl.BlockSpec(part, lambda t: (0, t, 0))
        scratch = [pltpu.VMEM((1, HEADS, HD, tokens), jnp.float32)]
        scratch += [pltpu.VMEM((1, HEADS, tokens), jnp.float32)] * 2
    else:
        out_shape = [kept, kept_row, kept_row]
        out_specs = [keep, keep_row, keep_row]
        scratch = []
    return pl.pallas_call(
        functools.partial(attend_kernel, ids, first, last),
        grid=(tiles,),
        in_specs=in_specs,
        out_specs=out_specs,
        out_shape=out_shape,
        scratch_shapes=scratch,
        compiler_params=pltpu.CompilerParams(vmem_limit_bytes=56 << 20),
        cost_estimate=pl.CostEstimate(
            flops=cost * 1_000_000_000, bytes_accessed=cost * 3_000_000, transcendentals=0
        ),
    )(*operands)


def body(
    hidden,
    control,
    conv_weight,
    ctrl_proj,
    mod_gain,
    mod_shift,
    w_qkv,
    kv_stale,
    key_tiles,
    key_count,
):
    frames, rows, width, dmodel = hidden.shape
    tiles_dev = key_count.shape[2]
    cin = conv_weight.shape[0] // 27
    attn_width = HEADS * HD
    planes = frames * rows
    rim = with_halo(control, (("tm", 0), ("height", 1)), 1)
    rim, kv_stale = lax.optimization_barrier((rim, kv_stale))
    grid = rim.reshape(frames + 2, rows + 2, width, cin)
    grid = jnp.pad(grid, ((0, 0), (0, 0), (1, 1), (0, 0)))
    taps = [
        grid[i : i + frames, j : j + rows, k : k + width]
        for i in range(3)
        for j in range(3)
        for k in range(3)
    ]
    stacked = jnp.concatenate(taps, axis=-1).reshape(frames * rows * width, 27 * cin)
    conv = jnp.dot(stacked, conv_weight, preferred_element_type=jnp.float32)
    act = jax.nn.silu(conv).astype(jnp.bfloat16)
    mixed = hidden.reshape(frames * rows * width, dmodel).astype(jnp.float32) + jnp.dot(
        act, ctrl_proj, preferred_element_type=jnp.float32
    )
    center = mixed - jnp.mean(mixed, axis=-1, keepdims=True)
    spread = jnp.mean(center * center, axis=-1, keepdims=True)
    normed = (center * lax.rsqrt(spread + 1e-06) * mod_gain + mod_shift).astype(jnp.bfloat16)
    qkv = jnp.dot(normed, w_qkv, preferred_element_type=jnp.float32).astype(jnp.bfloat16)
    qkv_grid = qkv.reshape(frames, rows, width, 3 * attn_width)
    fresh_kv = qkv_grid[..., attn_width:]
    frame_idx = lax.axis_index("tm")
    row_idx = lax.axis_index("height")
    row_total = lax.axis_size("height")
    idents = key_tiles[0, 0]
    counts = key_count[0, 0]
    dframe = idents // (row_total * tiles_dev) - frame_idx
    drow = idents // tiles_dev % row_total - row_idx
    source = locate(dframe, drow, frame_idx)
    used = lax.broadcasted_iota(jnp.int32, idents.shape, 1) < counts[:, None]
    code = jnp.where(used, source * 4 + idents % tiles_dev, -1).reshape(-1)
    qkv = qkv.reshape(planes, width, 3 * attn_width)

    def add(state, cost, *sources, last=False):
        flat = [
            (which, tuple(part.reshape(planes, width, part.shape[-1]) for part in parts))
            for which, *parts in sources
        ]
        return attend(code, qkv, flat, state, last, cost)

    below, above, rows_before, rows_after, mate = nearest(kv_stale)
    state = add(None, 20, (0, kv_stale), (3, mate))
    below, above, state = lax.optimization_barrier((below, above, state))
    far_keys, far_values, cross_keys, cross_values, beside = second(below, above, frame_idx)
    near = [(1, rows_before), (2, rows_after), (4, below), (5, above)]
    state = add(state, 30, *near, (6, beside))
    cross_keys, state = lax.optimization_barrier((cross_keys, state))
    trade_keys, mate_keys = third(cross_keys)
    state = add(state, 15, (7, far_keys, far_values))
    cross_values, trade_keys, mate_keys, state = lax.optimization_barrier(
        (cross_values, trade_keys, mate_keys, state)
    )
    trade_values, mate_values = third(cross_values)
    state = add(state, 12, (8, cross_keys, cross_values), (9, mate_keys, mate_values))
    state = add(state, 8, (10, trade_keys, trade_values), last=True)
    return (state.reshape(frames, rows, width, attn_width), fresh_kv)


def solution(mesh):
    placed = (
        P("tm", "height", None, None),
        P("tm", "height", None),
        P(),
        P(),
        P(),
        P(),
        P(),
        P("tm", "height", None, None),
        P("tm", "height", None, None),
        P("tm", "height", None),
    )
    return jax.shard_map(
        body,
        mesh=mesh,
        in_specs=placed,
        out_specs=(P("tm", "height", None, None), P("tm", "height", None, None)),
        check_vma=False,
    )
```

```python
import functools

import jax
import jax.numpy as jnp
from jax import lax
from jax.experimental import pallas as pl
from jax.experimental.pallas import tpu as pltpu
from jax.sharding import PartitionSpec as P

HEADS = 12
HD = 128
LOG2E = 1.4426950408889634
AHEAD = 2
RING = 8


def around(device, step):
    return device // RING * RING + (device + step) % RING


def swap(parity):
    return [(i, i ^ 1) for i in range(2 * RING) if i % 2 == parity]


def ring_sides(kv):
    everyone = range(2 * RING)
    below = lax.ppermute(kv, "tm", [(i, around(i, 2)) for i in everyone])
    above = lax.ppermute(kv, "tm", [(i, around(i, -2)) for i in everyone])
    return below, above


def nearest(kv):
    rows_before = from_behind(kv, "height", 1)
    rows_after = from_behind(kv, "height", -1)
    mate = lax.ppermute(kv, "tm", swap(0) + swap(1))
    return rows_before, rows_after, mate


def second(below, above, frame_idx):
    everyone = range(2 * RING)
    half = below.shape[-1] // 2
    from_below = (frame_idx < 2) | (frame_idx == 12) | (frame_idx == 13)
    odd = frame_idx % 2 == 1
    parts = (
        below[..., :half],
        above[..., half:],
        jnp.where(from_below, below[..., :half], above[..., :half]),
        jnp.where(from_below, below[..., half:], above[..., half:]),
    )
    parts, below, above = lax.optimization_barrier((parts, below, above))
    below_keys, above_values, edge_keys, edge_values = parts
    over = [(0, 8), (1, 9), (2, 10), (3, 11), (12, 4), (13, 5), (14, 6), (15, 7)]
    far_keys = lax.ppermute(below_keys, "tm", [(i, around(i, 2)) for i in everyone])
    far_values = lax.ppermute(above_values, "tm", [(i, around(i, -2)) for i in everyone])
    cross_keys = lax.ppermute(edge_keys, "tm", over)
    cross_values = lax.ppermute(edge_values, "tm", over)
    beside = lax.ppermute(jnp.where(odd, below, above), "tm", swap(0) + swap(1))
    return far_keys, far_values, cross_keys, cross_values, beside


def third(cross):
    trade = [(8, 10), (9, 11), (10, 8), (11, 9), (4, 6), (5, 7), (6, 4), (7, 5)]
    return lax.ppermute(cross, "tm", trade), lax.ppermute(cross, "tm", [(9, 8), (6, 7)])


def locate(dframe, drow, frame_idx):
    odd = frame_idx % 2
    spot = frame_idx % RING // 2
    low, high = spot == 0, spot == RING // 2 - 1
    table = {
        -1: jnp.where(odd == 1, 3, jnp.where(low, 9, 6)),
        1: jnp.where(odd == 0, 3, jnp.where(high, 9, 6)),
        -2: jnp.where(low, 8, 4),
        2: jnp.where(high, 8, 5),
        -4: jnp.where(spot < 2, 10, 7),
        4: jnp.where(spot < 2, 7, 10),
    }
    source = jnp.where(drow == -1, 1, jnp.where(drow == 1, 2, 0))
    for step, place in table.items():
        source = jnp.where(dframe == step, place, source)
    return source


def with_halo(cells, sides, width):
    for axis, dim in sides:
        count = lax.axis_size(axis)
        ends = count - 1
        head = lax.slice_in_dim(cells, 0, width, axis=dim)
        tail = lax.slice_in_dim(cells, cells.shape[dim] - width, cells.shape[dim], axis=dim)
        cells = jnp.concatenate(
            [
                lax.ppermute(tail, axis, [(i, (i + 1) % count) for i in range(ends)]),
                cells,
                lax.ppermute(head, axis, [((i + 1) % count, i) for i in range(ends)]),
            ],
            axis=dim,
        )
    return cells


def from_behind(block, axis, distance):
    devices = range(lax.axis_size(axis))
    route = [(i - distance, i) for i in devices if i - distance in devices]
    return lax.ppermute(block, axis, route)


def attend_kernel(ids, first, last, *refs):
    code_ref, q_ref = refs[0], refs[1]
    count = sum(n for _, n in ids)
    rest = refs[2 + count :]
    stale = []
    at = 2
    for which, n in ids:
        stale.append((which, refs[at], refs[at + n - 1], n == 1))
        at += n
    if not first:
        acc_in, top_in, sum_in = rest[:3]
        rest = rest[3:]
    if last:
        out_ref, acc, top, total = rest
    else:
        acc, top, total = rest
    planes, cols = q_ref.shape[0], q_ref.shape[1]
    tokens = planes * cols
    width = HEADS * HD
    tile = pl.program_id(0)
    scale = HD**-0.5 * LOG2E

    def add_tile(key_of, value_of, fresh):
        def scores(head):
            query = q_ref[:, :, head * HD : (head + 1) * HD].reshape(tokens, HD)
            return lax.dot_general(
                key_of(head), query, (((1,), (1,)), ((), ())), preferred_element_type=jnp.float32
            )

        ready = [scores(head) for head in range(AHEAD)]
        for head in range(HEADS):
            if head + AHEAD < HEADS:
                ready.append(scores(head + AHEAD))
            s = ready[head]
            new = jnp.max(s, axis=0, keepdims=True)
            if not fresh:
                old = top[0, head : head + 1]
                new = jnp.maximum(old, new)
                alpha = jnp.exp2((old - new) * scale)
            p = jnp.exp2((s - new) * scale)
            gain = jnp.sum(p, axis=0, keepdims=True)
            got = lax.dot_general(
                value_of(head),
                p.astype(jnp.bfloat16),
                (((0,), (0,)), ((), ())),
                preferred_element_type=jnp.float32,
            )
            if not fresh:
                gain = total[0, head : head + 1] * alpha + gain
                got = acc[0, head] * alpha + got
            top[0, head : head + 1] = new
            total[0, head : head + 1] = gain
            acc[0, head] = got

    if first:

        def fresh_part(low):
            return q_ref[:, :, low : low + HD].reshape(tokens, HD)

        add_tile(
            lambda head: fresh_part(width + head * HD),
            lambda head: fresh_part(2 * width + head * HD),
            True,
        )
    else:
        acc[...] = acc_in[...]
        top[...] = top_in[...]
        total[...] = sum_in[...]

    def slot(place, carry):
        code = code_ref[tile * 8 + place]
        for which, key_ref, value_ref, joined in stale:

            @pl.when(code >> 2 == which)
            def _():
                here = pl.ds(pl.multiple_of((code & 3) * cols, cols), cols)
                shift = width if joined else 0

                def key_of(head):
                    low = head * HD
                    return key_ref[:, here, low : low + HD].reshape(tokens, HD)

                def value_of(head):
                    low = shift + head * HD
                    return value_ref[:, here, low : low + HD].reshape(tokens, HD)

                add_tile(key_of, value_of, False)

        return carry

    lax.fori_loop(0, 8, slot, 0)
    if last:
        for head in range(HEADS):
            res = acc[0, head] / total[0, head : head + 1]
            res = jnp.transpose(res).astype(jnp.bfloat16)
            out_ref[:, :, head * HD : (head + 1) * HD] = res.reshape(planes, cols, HD)


def attend(code, qkv, sources, state, last, cost):
    ids = tuple((which, len(blocks)) for which, blocks in sources)
    blocks = [block for _, parts in sources for block in parts]
    planes, width, full = qkv.shape
    tiles = code.shape[0] // 8
    cols = width // tiles
    tokens = planes * cols
    first = state is None
    keep = pl.BlockSpec((1, HEADS, HD, tokens), lambda t: (t, 0, 0, 0))
    keep_row = pl.BlockSpec((1, HEADS, tokens), lambda t: (t, 0, 0))

    def whole(block):
        once = pl.Buffered(1)
        return pl.BlockSpec(block.shape, lambda t: (0, 0, 0), pipeline_mode=once)

    part = (planes, cols, HEADS * HD)
    qpart = (planes, cols, full) if first else part
    in_specs = [pl.BlockSpec(memory_space=pltpu.SMEM), pl.BlockSpec(qpart, lambda t: (0, t, 0))]
    in_specs += [whole(block) for block in blocks]
    operands = [code, qkv] + blocks
    if not first:
        in_specs += [keep, keep_row, keep_row]
        operands += list(state)
    kept = jax.ShapeDtypeStruct((tiles, HEADS, HD, tokens), jnp.float32)
    kept_row = jax.ShapeDtypeStruct((tiles, HEADS, tokens), jnp.float32)
    if last:
        out_shape = jax.ShapeDtypeStruct((planes, width, HEADS * HD), jnp.bfloat16)
        out_specs = pl.BlockSpec(part, lambda t: (0, t, 0))
        scratch = [pltpu.VMEM((1, HEADS, HD, tokens), jnp.float32)]
        scratch += [pltpu.VMEM((1, HEADS, tokens), jnp.float32)] * 2
    else:
        out_shape = [kept, kept_row, kept_row]
        out_specs = [keep, keep_row, keep_row]
        scratch = []
    return pl.pallas_call(
        functools.partial(attend_kernel, ids, first, last),
        grid=(tiles,),
        in_specs=in_specs,
        out_specs=out_specs,
        out_shape=out_shape,
        scratch_shapes=scratch,
        compiler_params=pltpu.CompilerParams(vmem_limit_bytes=56 << 20),
        cost_estimate=pl.CostEstimate(
            flops=cost * 1_000_000_000, bytes_accessed=cost * 3_000_000, transcendentals=0
        ),
    )(*operands)


def body(
    hidden,
    control,
    conv_weight,
    ctrl_proj,
    mod_gain,
    mod_shift,
    w_qkv,
    kv_stale,
    key_tiles,
    key_count,
):
    frames, rows, width, dmodel = hidden.shape
    tiles_dev = key_count.shape[2]
    cin = conv_weight.shape[0] // 27
    attn_width = HEADS * HD
    planes = frames * rows
    rim = with_halo(control, (("tm", 0),), 1)
    rim, kv_stale = lax.optimization_barrier((rim, kv_stale))
    below, above = ring_sides(kv_stale)
    rim = with_halo(rim, (("height", 1),), 1)
    rim, kv_late = lax.optimization_barrier((rim, kv_stale))
    rows_before, rows_after, mate = nearest(kv_late)
    grid = rim.reshape(frames + 2, rows + 2, width, cin)
    grid = jnp.pad(grid, ((0, 0), (0, 0), (1, 1), (0, 0)))
    taps = [
        grid[i : i + frames, j : j + rows, k : k + width]
        for i in range(3)
        for j in range(3)
        for k in range(3)
    ]
    stacked = jnp.concatenate(taps, axis=-1).reshape(frames * rows * width, 27 * cin)
    conv = jnp.dot(stacked, conv_weight, preferred_element_type=jnp.float32)
    act = jax.nn.silu(conv).astype(jnp.bfloat16)
    mixed = hidden.reshape(frames * rows * width, dmodel).astype(jnp.float32) + jnp.dot(
        act, ctrl_proj, preferred_element_type=jnp.float32
    )
    center = mixed - jnp.mean(mixed, axis=-1, keepdims=True)
    spread = jnp.mean(center * center, axis=-1, keepdims=True)
    normed = (center * lax.rsqrt(spread + 1e-06) * mod_gain + mod_shift).astype(jnp.bfloat16)
    qkv = jnp.dot(normed, w_qkv, preferred_element_type=jnp.float32).astype(jnp.bfloat16)
    qkv_grid = qkv.reshape(frames, rows, width, 3 * attn_width)
    fresh_kv = qkv_grid[..., attn_width:]
    frame_idx = lax.axis_index("tm")
    row_idx = lax.axis_index("height")
    row_total = lax.axis_size("height")
    idents = key_tiles[0, 0]
    counts = key_count[0, 0]
    dframe = idents // (row_total * tiles_dev) - frame_idx
    drow = idents // tiles_dev % row_total - row_idx
    source = locate(dframe, drow, frame_idx)
    used = lax.broadcasted_iota(jnp.int32, idents.shape, 1) < counts[:, None]
    code = jnp.where(used, source * 4 + idents % tiles_dev, -1).reshape(-1)
    qkv = qkv.reshape(planes, width, 3 * attn_width)

    def add(state, cost, *sources, last=False):
        flat = [
            (which, tuple(part.reshape(planes, width, part.shape[-1]) for part in parts))
            for which, *parts in sources
        ]
        return attend(code, qkv, flat, state, last, cost)

    state = add(None, 20, (0, kv_stale), (3, mate))
    below, above, state = lax.optimization_barrier((below, above, state))
    far_keys, far_values, cross_keys, cross_values, beside = second(below, above, frame_idx)
    near = [(1, rows_before), (2, rows_after), (4, below), (5, above)]
    state = add(state, 30, *near, (6, beside))
    cross_keys, state = lax.optimization_barrier((cross_keys, state))
    trade_keys, mate_keys = third(cross_keys)
    state = add(state, 15, (7, far_keys, far_values))
    cross_values, trade_keys, mate_keys, state = lax.optimization_barrier(
        (cross_values, trade_keys, mate_keys, state)
    )
    trade_values, mate_values = third(cross_values)
    state = add(state, 12, (8, cross_keys, cross_values), (9, mate_keys, mate_values))
    state = add(state, 8, (10, trade_keys, trade_values), last=True)
    return (state.reshape(frames, rows, width, attn_width), fresh_kv)


def solution(mesh):
    placed = (
        P("tm", "height", None, None),
        P("tm", "height", None),
        P(),
        P(),
        P(),
        P(),
        P(),
        P("tm", "height", None, None),
        P("tm", "height", None, None),
        P("tm", "height", None),
    )
    return jax.shard_map(
        body,
        mesh=mesh,
        in_specs=placed,
        out_specs=(P("tm", "height", None, None), P("tm", "height", None, None)),
        check_vma=False,
    )
```

```python
import functools

import jax
import jax.numpy as jnp
from jax import lax
from jax.experimental import pallas as pl
from jax.experimental.pallas import tpu as pltpu
from jax.sharding import PartitionSpec as P

HEADS = 12
HD = 128
LOG2E = 1.4426950408889634
AHEAD = 2
RING = 8


def around(device, step):
    return device // RING * RING + (device + step) % RING


def swap(parity):
    return [(i, i ^ 1) for i in range(2 * RING) if i % 2 == parity]


def ring_sides(kv):
    everyone = range(2 * RING)
    below = lax.ppermute(kv, "tm", [(i, around(i, 2)) for i in everyone])
    above = lax.ppermute(kv, "tm", [(i, around(i, -2)) for i in everyone])
    return below, above


def nearest(kv):
    rows_before = from_behind(kv, "height", 1)
    rows_after = from_behind(kv, "height", -1)
    mate = lax.ppermute(kv, "tm", swap(0) + swap(1))
    return rows_before, rows_after, mate


def second(below, above, frame_idx):
    everyone = range(2 * RING)
    half = below.shape[-1] // 2
    from_below = (frame_idx < 2) | (frame_idx == 12) | (frame_idx == 13)
    odd = frame_idx % 2 == 1
    edge_keys = jnp.where(from_below, below[..., :half], above[..., :half])
    edge_keys, below, above = lax.optimization_barrier((edge_keys, below, above))
    edge_values = jnp.where(from_below, below[..., half:], above[..., half:])
    parts = (edge_values, below[..., :half], above[..., half:])
    parts, below, above = lax.optimization_barrier((parts, below, above))
    edge_values, below_keys, above_values = parts
    over = [(0, 8), (1, 9), (2, 10), (3, 11), (12, 4), (13, 5), (14, 6), (15, 7)]
    cross_keys = lax.ppermute(edge_keys, "tm", over)
    cross_values = lax.ppermute(edge_values, "tm", over)
    far_keys = lax.ppermute(below_keys, "tm", [(i, around(i, 2)) for i in everyone])
    far_values = lax.ppermute(above_values, "tm", [(i, around(i, -2)) for i in everyone])
    beside = lax.ppermute(jnp.where(odd, below, above), "tm", swap(0) + swap(1))
    return far_keys, far_values, cross_keys, cross_values, beside


def third(cross):
    trade = [(8, 10), (9, 11), (10, 8), (11, 9), (4, 6), (5, 7), (6, 4), (7, 5)]
    return lax.ppermute(cross, "tm", trade), lax.ppermute(cross, "tm", [(9, 8), (6, 7)])


def locate(dframe, drow, frame_idx):
    odd = frame_idx % 2
    spot = frame_idx % RING // 2
    low, high = spot == 0, spot == RING // 2 - 1
    table = {
        -1: jnp.where(odd == 1, 3, jnp.where(low, 9, 6)),
        1: jnp.where(odd == 0, 3, jnp.where(high, 9, 6)),
        -2: jnp.where(low, 8, 4),
        2: jnp.where(high, 8, 5),
        -4: jnp.where(spot < 2, 10, 7),
        4: jnp.where(spot < 2, 7, 10),
    }
    source = jnp.where(drow == -1, 1, jnp.where(drow == 1, 2, 0))
    for step, place in table.items():
        source = jnp.where(dframe == step, place, source)
    return source


def with_halo(cells, sides, width):
    for axis, dim in sides:
        count = lax.axis_size(axis)
        ends = count - 1
        head = lax.slice_in_dim(cells, 0, width, axis=dim)
        tail = lax.slice_in_dim(cells, cells.shape[dim] - width, cells.shape[dim], axis=dim)
        cells = jnp.concatenate(
            [
                lax.ppermute(tail, axis, [(i, (i + 1) % count) for i in range(ends)]),
                cells,
                lax.ppermute(head, axis, [((i + 1) % count, i) for i in range(ends)]),
            ],
            axis=dim,
        )
    return cells


def from_behind(block, axis, distance):
    devices = range(lax.axis_size(axis))
    route = [(i - distance, i) for i in devices if i - distance in devices]
    return lax.ppermute(block, axis, route)


def attend_kernel(ids, first, last, *refs):
    code_ref, q_ref = refs[0], refs[1]
    count = sum(n for _, n in ids)
    rest = refs[2 + count :]
    stale = []
    at = 2
    for which, n in ids:
        stale.append((which, refs[at], refs[at + n - 1], n == 1))
        at += n
    if not first:
        acc_in, top_in, sum_in = rest[:3]
        rest = rest[3:]
    if last:
        out_ref, acc, top, total = rest
    else:
        acc, top, total = rest
    planes, cols = q_ref.shape[0], q_ref.shape[1]
    tokens = planes * cols
    width = HEADS * HD
    tile = pl.program_id(0)
    scale = HD**-0.5 * LOG2E

    def add_tile(key_of, value_of, fresh):
        def scores(head):
            query = q_ref[:, :, head * HD : (head + 1) * HD].reshape(tokens, HD)
            return lax.dot_general(
                key_of(head), query, (((1,), (1,)), ((), ())), preferred_element_type=jnp.float32
            )

        ready = [scores(head) for head in range(AHEAD)]
        for head in range(HEADS):
            if head + AHEAD < HEADS:
                ready.append(scores(head + AHEAD))
            s = ready[head]
            new = jnp.max(s, axis=0, keepdims=True)
            if not fresh:
                old = top[0, head : head + 1]
                new = jnp.maximum(old, new)
                alpha = jnp.exp2((old - new) * scale)
            p = jnp.exp2((s - new) * scale)
            gain = jnp.sum(p, axis=0, keepdims=True)
            got = lax.dot_general(
                value_of(head),
                p.astype(jnp.bfloat16),
                (((0,), (0,)), ((), ())),
                preferred_element_type=jnp.float32,
            )
            if not fresh:
                gain = total[0, head : head + 1] * alpha + gain
                got = acc[0, head] * alpha + got
            top[0, head : head + 1] = new
            total[0, head : head + 1] = gain
            acc[0, head] = got

    if first:

        def fresh_part(low):
            return q_ref[:, :, low : low + HD].reshape(tokens, HD)

        add_tile(
            lambda head: fresh_part(width + head * HD),
            lambda head: fresh_part(2 * width + head * HD),
            True,
        )
    else:
        acc[...] = acc_in[...]
        top[...] = top_in[...]
        total[...] = sum_in[...]

    def slot(place, carry):
        code = code_ref[tile * 8 + place]
        for which, key_ref, value_ref, joined in stale:

            @pl.when(code >> 2 == which)
            def _():
                here = pl.ds(pl.multiple_of((code & 3) * cols, cols), cols)
                shift = width if joined else 0

                def key_of(head):
                    low = head * HD
                    return key_ref[:, here, low : low + HD].reshape(tokens, HD)

                def value_of(head):
                    low = shift + head * HD
                    return value_ref[:, here, low : low + HD].reshape(tokens, HD)

                add_tile(key_of, value_of, False)

        return carry

    lax.fori_loop(0, 8, slot, 0)
    if last:
        for head in range(HEADS):
            res = acc[0, head] / total[0, head : head + 1]
            res = jnp.transpose(res).astype(jnp.bfloat16)
            out_ref[:, :, head * HD : (head + 1) * HD] = res.reshape(planes, cols, HD)


def attend(code, qkv, sources, state, last, cost):
    ids = tuple((which, len(blocks)) for which, blocks in sources)
    blocks = [block for _, parts in sources for block in parts]
    planes, width, full = qkv.shape
    tiles = code.shape[0] // 8
    cols = width // tiles
    tokens = planes * cols
    first = state is None
    keep = pl.BlockSpec((1, HEADS, HD, tokens), lambda t: (t, 0, 0, 0))
    keep_row = pl.BlockSpec((1, HEADS, tokens), lambda t: (t, 0, 0))

    def whole(block):
        once = pl.Buffered(1)
        return pl.BlockSpec(block.shape, lambda t: (0, 0, 0), pipeline_mode=once)

    part = (planes, cols, HEADS * HD)
    qpart = (planes, cols, full) if first else part
    in_specs = [pl.BlockSpec(memory_space=pltpu.SMEM), pl.BlockSpec(qpart, lambda t: (0, t, 0))]
    in_specs += [whole(block) for block in blocks]
    operands = [code, qkv] + blocks
    if not first:
        in_specs += [keep, keep_row, keep_row]
        operands += list(state)
    kept = jax.ShapeDtypeStruct((tiles, HEADS, HD, tokens), jnp.float32)
    kept_row = jax.ShapeDtypeStruct((tiles, HEADS, tokens), jnp.float32)
    if last:
        out_shape = jax.ShapeDtypeStruct((planes, width, HEADS * HD), jnp.bfloat16)
        out_specs = pl.BlockSpec(part, lambda t: (0, t, 0))
        scratch = [pltpu.VMEM((1, HEADS, HD, tokens), jnp.float32)]
        scratch += [pltpu.VMEM((1, HEADS, tokens), jnp.float32)] * 2
    else:
        out_shape = [kept, kept_row, kept_row]
        out_specs = [keep, keep_row, keep_row]
        scratch = []
    return pl.pallas_call(
        functools.partial(attend_kernel, ids, first, last),
        grid=(tiles,),
        in_specs=in_specs,
        out_specs=out_specs,
        out_shape=out_shape,
        scratch_shapes=scratch,
        compiler_params=pltpu.CompilerParams(vmem_limit_bytes=56 << 20),
        cost_estimate=pl.CostEstimate(
            flops=cost * 1_000_000_000, bytes_accessed=cost * 3_000_000, transcendentals=0
        ),
    )(*operands)


def body(
    hidden,
    control,
    conv_weight,
    ctrl_proj,
    mod_gain,
    mod_shift,
    w_qkv,
    kv_stale,
    key_tiles,
    key_count,
):
    frames, rows, width, dmodel = hidden.shape
    tiles_dev = key_count.shape[2]
    cin = conv_weight.shape[0] // 27
    attn_width = HEADS * HD
    planes = frames * rows
    rim = with_halo(control, (("tm", 0),), 1)
    rim, kv_stale = lax.optimization_barrier((rim, kv_stale))
    below, above = ring_sides(kv_stale)
    rim = with_halo(rim, (("height", 1),), 1)
    rim, kv_late = lax.optimization_barrier((rim, kv_stale))
    rows_before, rows_after, mate = nearest(kv_late)
    grid = rim.reshape(frames + 2, rows + 2, width, cin)
    grid = jnp.pad(grid, ((0, 0), (0, 0), (1, 1), (0, 0)))
    taps = [
        grid[i : i + frames, j : j + rows, k : k + width]
        for i in range(3)
        for j in range(3)
        for k in range(3)
    ]
    stacked = jnp.concatenate(taps, axis=-1).reshape(frames * rows * width, 27 * cin)
    conv = jnp.dot(stacked, conv_weight, preferred_element_type=jnp.float32)
    act = jax.nn.silu(conv).astype(jnp.bfloat16)
    mixed = hidden.reshape(frames * rows * width, dmodel).astype(jnp.float32) + jnp.dot(
        act, ctrl_proj, preferred_element_type=jnp.float32
    )
    center = mixed - jnp.mean(mixed, axis=-1, keepdims=True)
    spread = jnp.mean(center * center, axis=-1, keepdims=True)
    normed = (center * lax.rsqrt(spread + 1e-06) * mod_gain + mod_shift).astype(jnp.bfloat16)
    qkv = jnp.dot(normed, w_qkv, preferred_element_type=jnp.float32).astype(jnp.bfloat16)
    qkv_grid = qkv.reshape(frames, rows, width, 3 * attn_width)
    fresh_kv = qkv_grid[..., attn_width:]
    frame_idx = lax.axis_index("tm")
    row_idx = lax.axis_index("height")
    row_total = lax.axis_size("height")
    idents = key_tiles[0, 0]
    counts = key_count[0, 0]
    dframe = idents // (row_total * tiles_dev) - frame_idx
    drow = idents // tiles_dev % row_total - row_idx
    source = locate(dframe, drow, frame_idx)
    used = lax.broadcasted_iota(jnp.int32, idents.shape, 1) < counts[:, None]
    code = jnp.where(used, source * 4 + idents % tiles_dev, -1).reshape(-1)
    qkv = qkv.reshape(planes, width, 3 * attn_width)

    def add(state, cost, *sources, last=False):
        flat = [
            (which, tuple(part.reshape(planes, width, part.shape[-1]) for part in parts))
            for which, *parts in sources
        ]
        return attend(code, qkv, flat, state, last, cost)

    state = add(None, 20, (0, kv_stale), (3, mate))
    below, above, state = lax.optimization_barrier((below, above, state))
    far_keys, far_values, cross_keys, cross_values, beside = second(below, above, frame_idx)
    near = [(1, rows_before), (2, rows_after), (4, below), (5, above)]
    state = add(state, 30, *near, (6, beside))
    cross_keys, state = lax.optimization_barrier((cross_keys, state))
    trade_keys, mate_keys = third(cross_keys)
    state = add(state, 15, (7, far_keys, far_values))
    cross_values, trade_keys, mate_keys, state = lax.optimization_barrier(
        (cross_values, trade_keys, mate_keys, state)
    )
    trade_values, mate_values = third(cross_values)
    state = add(state, 12, (8, cross_keys, cross_values), (9, mate_keys, mate_values))
    state = add(state, 8, (10, trade_keys, trade_values), last=True)
    return (state.reshape(frames, rows, width, attn_width), fresh_kv)


def solution(mesh):
    placed = (
        P("tm", "height", None, None),
        P("tm", "height", None),
        P(),
        P(),
        P(),
        P(),
        P(),
        P("tm", "height", None, None),
        P("tm", "height", None, None),
        P("tm", "height", None),
    )
    return jax.shard_map(
        body,
        mesh=mesh,
        in_specs=placed,
        out_specs=(P("tm", "height", None, None), P("tm", "height", None, None)),
        check_vma=False,
    )
```

```python
import functools

import jax
import jax.numpy as jnp
from jax import lax
from jax.experimental import pallas as pl
from jax.experimental.pallas import tpu as pltpu
from jax.sharding import PartitionSpec as P

HEADS = 12
HD = 128
LOG2E = 1.4426950408889634
AHEAD = 2
RING = 8


def around(device, step):
    return device // RING * RING + (device + step) % RING


def swap(parity):
    return [(i, i ^ 1) for i in range(2 * RING) if i % 2 == parity]


def ring_sides(kv):
    everyone = range(2 * RING)
    below = lax.ppermute(kv, "tm", [(i, around(i, 2)) for i in everyone])
    above = lax.ppermute(kv, "tm", [(i, around(i, -2)) for i in everyone])
    return below, above


def nearest(kv):
    rows_before = from_behind(kv, "height", 1)
    rows_after = from_behind(kv, "height", -1)
    mate = lax.ppermute(kv, "tm", swap(0) + swap(1))
    return rows_before, rows_after, mate


def second(below, above, rows_before, rows_after, frame_idx):
    everyone = range(2 * RING)
    half = below.shape[-1] // 2
    from_below = (frame_idx < 2) | (frame_idx == 12) | (frame_idx == 13)
    odd = frame_idx % 2 == 1
    parts = (
        jnp.where(from_below, below[..., :half], above[..., :half]),
        below[..., :half],
        above[..., half:],
    )
    parts, below, above = lax.optimization_barrier((parts, below, above))
    edge_keys, below_keys, above_values = parts
    over = [(0, 8), (1, 9), (2, 10), (3, 11), (12, 4), (13, 5), (14, 6), (15, 7)]
    cross_keys = lax.ppermute(edge_keys, "tm", over)
    far_keys = lax.ppermute(below_keys, "tm", [(i, around(i, 2)) for i in everyone])
    far_values = lax.ppermute(above_values, "tm", [(i, around(i, -2)) for i in everyone])
    below, above, rows_before, rows_after = lax.optimization_barrier(
        (below, above, rows_before, rows_after)
    )
    edge_values = jnp.where(from_below, below[..., half:], above[..., half:])
    cross_values = lax.ppermute(edge_values, "tm", over)
    beside = lax.ppermute(jnp.where(odd, below, above), "tm", swap(0) + swap(1))
    rows = (rows_before, rows_after)
    return far_keys, far_values, cross_keys, cross_values, beside, rows


def third(cross):
    trade = [(8, 10), (9, 11), (10, 8), (11, 9), (4, 6), (5, 7), (6, 4), (7, 5)]
    return lax.ppermute(cross, "tm", trade), lax.ppermute(cross, "tm", [(9, 8), (6, 7)])


def locate(dframe, drow, frame_idx):
    odd = frame_idx % 2
    spot = frame_idx % RING // 2
    low, high = spot == 0, spot == RING // 2 - 1
    table = {
        -1: jnp.where(odd == 1, 3, jnp.where(low, 9, 6)),
        1: jnp.where(odd == 0, 3, jnp.where(high, 9, 6)),
        -2: jnp.where(low, 8, 4),
        2: jnp.where(high, 8, 5),
        -4: jnp.where(spot < 2, 10, 7),
        4: jnp.where(spot < 2, 7, 10),
    }
    source = jnp.where(drow == -1, 1, jnp.where(drow == 1, 2, 0))
    for step, place in table.items():
        source = jnp.where(dframe == step, place, source)
    return source


def with_halo(cells, sides, width):
    for axis, dim in sides:
        count = lax.axis_size(axis)
        ends = count - 1
        head = lax.slice_in_dim(cells, 0, width, axis=dim)
        tail = lax.slice_in_dim(cells, cells.shape[dim] - width, cells.shape[dim], axis=dim)
        cells = jnp.concatenate(
            [
                lax.ppermute(tail, axis, [(i, (i + 1) % count) for i in range(ends)]),
                cells,
                lax.ppermute(head, axis, [((i + 1) % count, i) for i in range(ends)]),
            ],
            axis=dim,
        )
    return cells


def from_behind(block, axis, distance):
    devices = range(lax.axis_size(axis))
    route = [(i - distance, i) for i in devices if i - distance in devices]
    return lax.ppermute(block, axis, route)


def attend_kernel(ids, first, last, *refs):
    code_ref, q_ref = refs[0], refs[1]
    count = sum(n for _, n in ids)
    rest = refs[2 + count :]
    stale = []
    at = 2
    for which, n in ids:
        stale.append((which, refs[at], refs[at + n - 1], n == 1))
        at += n
    if not first:
        acc_in, top_in, sum_in = rest[:3]
        rest = rest[3:]
    if last:
        out_ref, acc, top, total = rest
    else:
        acc, top, total = rest
    planes, cols = q_ref.shape[0], q_ref.shape[1]
    tokens = planes * cols
    width = HEADS * HD
    tile = pl.program_id(0)
    scale = HD**-0.5 * LOG2E

    def add_tile(key_of, value_of, fresh):
        def scores(head):
            query = q_ref[:, :, head * HD : (head + 1) * HD].reshape(tokens, HD)
            return lax.dot_general(
                key_of(head), query, (((1,), (1,)), ((), ())), preferred_element_type=jnp.float32
            )

        ready = [scores(head) for head in range(AHEAD)]
        for head in range(HEADS):
            if head + AHEAD < HEADS:
                ready.append(scores(head + AHEAD))
            s = ready[head]
            new = jnp.max(s, axis=0, keepdims=True)
            if not fresh:
                old = top[0, head : head + 1]
                new = jnp.maximum(old, new)
                alpha = jnp.exp2((old - new) * scale)
            p = jnp.exp2((s - new) * scale)
            gain = jnp.sum(p, axis=0, keepdims=True)
            got = lax.dot_general(
                value_of(head),
                p.astype(jnp.bfloat16),
                (((0,), (0,)), ((), ())),
                preferred_element_type=jnp.float32,
            )
            if not fresh:
                gain = total[0, head : head + 1] * alpha + gain
                got = acc[0, head] * alpha + got
            top[0, head : head + 1] = new
            total[0, head : head + 1] = gain
            acc[0, head] = got

    if first:

        def fresh_part(low):
            return q_ref[:, :, low : low + HD].reshape(tokens, HD)

        add_tile(
            lambda head: fresh_part(width + head * HD),
            lambda head: fresh_part(2 * width + head * HD),
            True,
        )
    else:
        acc[...] = acc_in[...]
        top[...] = top_in[...]
        total[...] = sum_in[...]

    def slot(place, carry):
        code = code_ref[tile * 8 + place]
        for which, key_ref, value_ref, joined in stale:

            @pl.when(code >> 2 == which)
            def _():
                here = pl.ds(pl.multiple_of((code & 3) * cols, cols), cols)
                shift = width if joined else 0

                def key_of(head):
                    low = head * HD
                    return key_ref[:, here, low : low + HD].reshape(tokens, HD)

                def value_of(head):
                    low = shift + head * HD
                    return value_ref[:, here, low : low + HD].reshape(tokens, HD)

                add_tile(key_of, value_of, False)

        return carry

    lax.fori_loop(0, 8, slot, 0)
    if last:
        for head in range(HEADS):
            res = acc[0, head] / total[0, head : head + 1]
            res = jnp.transpose(res).astype(jnp.bfloat16)
            out_ref[:, :, head * HD : (head + 1) * HD] = res.reshape(planes, cols, HD)


def attend(code, qkv, sources, state, last, cost):
    ids = tuple((which, len(blocks)) for which, blocks in sources)
    blocks = [block for _, parts in sources for block in parts]
    planes, width, full = qkv.shape
    tiles = code.shape[0] // 8
    cols = width // tiles
    tokens = planes * cols
    first = state is None
    keep = pl.BlockSpec((1, HEADS, HD, tokens), lambda t: (t, 0, 0, 0))
    keep_row = pl.BlockSpec((1, HEADS, tokens), lambda t: (t, 0, 0))

    def whole(block):
        once = pl.Buffered(1)
        return pl.BlockSpec(block.shape, lambda t: (0, 0, 0), pipeline_mode=once)

    part = (planes, cols, HEADS * HD)
    qpart = (planes, cols, full) if first else part
    in_specs = [pl.BlockSpec(memory_space=pltpu.SMEM), pl.BlockSpec(qpart, lambda t: (0, t, 0))]
    in_specs += [whole(block) for block in blocks]
    operands = [code, qkv] + blocks
    if not first:
        in_specs += [keep, keep_row, keep_row]
        operands += list(state)
    kept = jax.ShapeDtypeStruct((tiles, HEADS, HD, tokens), jnp.float32)
    kept_row = jax.ShapeDtypeStruct((tiles, HEADS, tokens), jnp.float32)
    if last:
        out_shape = jax.ShapeDtypeStruct((planes, width, HEADS * HD), jnp.bfloat16)
        out_specs = pl.BlockSpec(part, lambda t: (0, t, 0))
        scratch = [pltpu.VMEM((1, HEADS, HD, tokens), jnp.float32)]
        scratch += [pltpu.VMEM((1, HEADS, tokens), jnp.float32)] * 2
    else:
        out_shape = [kept, kept_row, kept_row]
        out_specs = [keep, keep_row, keep_row]
        scratch = []
    return pl.pallas_call(
        functools.partial(attend_kernel, ids, first, last),
        grid=(tiles,),
        in_specs=in_specs,
        out_specs=out_specs,
        out_shape=out_shape,
        scratch_shapes=scratch,
        compiler_params=pltpu.CompilerParams(vmem_limit_bytes=56 << 20),
        cost_estimate=pl.CostEstimate(
            flops=cost * 1_000_000_000, bytes_accessed=cost * 3_000_000, transcendentals=0
        ),
    )(*operands)


def body(
    hidden,
    control,
    conv_weight,
    ctrl_proj,
    mod_gain,
    mod_shift,
    w_qkv,
    kv_stale,
    key_tiles,
    key_count,
):
    frames, rows, width, dmodel = hidden.shape
    tiles_dev = key_count.shape[2]
    cin = conv_weight.shape[0] // 27
    attn_width = HEADS * HD
    planes = frames * rows
    rim = with_halo(control, (("tm", 0),), 1)
    rim, kv_stale = lax.optimization_barrier((rim, kv_stale))
    below, above = ring_sides(kv_stale)
    rim = with_halo(rim, (("height", 1),), 1)
    rim, kv_late = lax.optimization_barrier((rim, kv_stale))
    rows_before, rows_after, mate = nearest(kv_late)
    grid = rim.reshape(frames + 2, rows + 2, width, cin)
    grid = jnp.pad(grid, ((0, 0), (0, 0), (1, 1), (0, 0)))
    taps = [
        grid[i : i + frames, j : j + rows, k : k + width]
        for i in range(3)
        for j in range(3)
        for k in range(3)
    ]
    stacked = jnp.concatenate(taps, axis=-1).reshape(frames * rows * width, 27 * cin)
    conv = jnp.dot(stacked, conv_weight, preferred_element_type=jnp.float32)
    act = jax.nn.silu(conv).astype(jnp.bfloat16)
    mixed = hidden.reshape(frames * rows * width, dmodel).astype(jnp.float32) + jnp.dot(
        act, ctrl_proj, preferred_element_type=jnp.float32
    )
    center = mixed - jnp.mean(mixed, axis=-1, keepdims=True)
    spread = jnp.mean(center * center, axis=-1, keepdims=True)
    normed = (center * lax.rsqrt(spread + 1e-06) * mod_gain + mod_shift).astype(jnp.bfloat16)
    qkv = jnp.dot(normed, w_qkv, preferred_element_type=jnp.float32).astype(jnp.bfloat16)
    qkv_grid = qkv.reshape(frames, rows, width, 3 * attn_width)
    fresh_kv = qkv_grid[..., attn_width:]
    frame_idx = lax.axis_index("tm")
    row_idx = lax.axis_index("height")
    row_total = lax.axis_size("height")
    idents = key_tiles[0, 0]
    counts = key_count[0, 0]
    dframe = idents // (row_total * tiles_dev) - frame_idx
    drow = idents // tiles_dev % row_total - row_idx
    source = locate(dframe, drow, frame_idx)
    used = lax.broadcasted_iota(jnp.int32, idents.shape, 1) < counts[:, None]
    code = jnp.where(used, source * 4 + idents % tiles_dev, -1).reshape(-1)
    qkv = qkv.reshape(planes, width, 3 * attn_width)

    def add(state, cost, *sources, last=False):
        flat = [
            (which, tuple(part.reshape(planes, width, part.shape[-1]) for part in parts))
            for which, *parts in sources
        ]
        return attend(code, qkv, flat, state, last, cost)

    state = add(None, 20, (0, kv_stale), (3, mate))
    below, above, state = lax.optimization_barrier((below, above, state))
    far_keys, far_values, cross_keys, cross_values, beside, level = second(
        below, above, rows_before, rows_after, frame_idx
    )
    state = add(state, 25, (1, level[0]), (2, level[1]), (4, below), (5, above))
    cross_keys, state = lax.optimization_barrier((cross_keys, state))
    trade_keys, mate_keys = third(cross_keys)
    state = add(state, 20, (6, beside), (7, far_keys, far_values))
    cross_values, trade_keys, mate_keys, state = lax.optimization_barrier(
        (cross_values, trade_keys, mate_keys, state)
    )
    trade_values, mate_values = third(cross_values)
    state = add(state, 12, (8, cross_keys, cross_values), (9, mate_keys, mate_values))
    state = add(state, 8, (10, trade_keys, trade_values), last=True)
    return (state.reshape(frames, rows, width, attn_width), fresh_kv)


def solution(mesh):
    placed = (
        P("tm", "height", None, None),
        P("tm", "height", None),
        P(),
        P(),
        P(),
        P(),
        P(),
        P("tm", "height", None, None),
        P("tm", "height", None, None),
        P("tm", "height", None),
    )
    return jax.shard_map(
        body,
        mesh=mesh,
        in_specs=placed,
        out_specs=(P("tm", "height", None, None), P("tm", "height", None, None)),
        check_vma=False,
    )
```

```python
import functools

import jax
import jax.numpy as jnp
from jax import lax
from jax.experimental import pallas as pl
from jax.experimental.pallas import tpu as pltpu
from jax.sharding import PartitionSpec as P

HEADS = 12
HD = 128
LOG2E = 1.4426950408889634
AHEAD = 3
RING = 8


def around(device, step):
    return device // RING * RING + (device + step) % RING


def swap(parity):
    return [(i, i ^ 1) for i in range(2 * RING) if i % 2 == parity]


def ring_sides(kv):
    everyone = range(2 * RING)
    below = lax.ppermute(kv, "tm", [(i, around(i, 2)) for i in everyone])
    above = lax.ppermute(kv, "tm", [(i, around(i, -2)) for i in everyone])
    return below, above


def nearest(kv):
    rows_before = from_behind(kv, "height", 1)
    rows_after = from_behind(kv, "height", -1)
    mate = lax.ppermute(kv, "tm", swap(0) + swap(1))
    return rows_before, rows_after, mate


def second(below, above, frame_idx):
    everyone = range(2 * RING)
    half = below.shape[-1] // 2
    from_below = (frame_idx < 2) | (frame_idx == 12) | (frame_idx == 13)
    odd = frame_idx % 2 == 1
    parts = (
        below[..., :half],
        above[..., half:],
        jnp.where(from_below, below[..., :half], above[..., :half]),
        jnp.where(from_below, below[..., half:], above[..., half:]),
    )
    parts, below, above = lax.optimization_barrier((parts, below, above))
    below_keys, above_values, edge_keys, edge_values = parts
    over = [(0, 8), (1, 9), (2, 10), (3, 11), (12, 4), (13, 5), (14, 6), (15, 7)]
    far_keys = lax.ppermute(below_keys, "tm", [(i, around(i, 2)) for i in everyone])
    far_values = lax.ppermute(above_values, "tm", [(i, around(i, -2)) for i in everyone])
    cross_keys = lax.ppermute(edge_keys, "tm", over)
    cross_values = lax.ppermute(edge_values, "tm", over)
    beside = lax.ppermute(jnp.where(odd, below, above), "tm", swap(0) + swap(1))
    return far_keys, far_values, cross_keys, cross_values, beside


def third(cross):
    trade = [(8, 10), (9, 11), (10, 8), (11, 9), (4, 6), (5, 7), (6, 4), (7, 5)]
    return lax.ppermute(cross, "tm", trade), lax.ppermute(cross, "tm", [(9, 8), (6, 7)])


def locate(dframe, drow, frame_idx):
    odd = frame_idx % 2
    spot = frame_idx % RING // 2
    low, high = spot == 0, spot == RING // 2 - 1
    table = {
        -1: jnp.where(odd == 1, 3, jnp.where(low, 9, 6)),
        1: jnp.where(odd == 0, 3, jnp.where(high, 9, 6)),
        -2: jnp.where(low, 8, 4),
        2: jnp.where(high, 8, 5),
        -4: jnp.where(spot < 2, 10, 7),
        4: jnp.where(spot < 2, 7, 10),
    }
    source = jnp.where(drow == -1, 1, jnp.where(drow == 1, 2, 0))
    for step, place in table.items():
        source = jnp.where(dframe == step, place, source)
    return source


def with_halo(cells, sides, width):
    for axis, dim in sides:
        count = lax.axis_size(axis)
        ends = count - 1
        head = lax.slice_in_dim(cells, 0, width, axis=dim)
        tail = lax.slice_in_dim(cells, cells.shape[dim] - width, cells.shape[dim], axis=dim)
        cells = jnp.concatenate(
            [
                lax.ppermute(tail, axis, [(i, (i + 1) % count) for i in range(ends)]),
                cells,
                lax.ppermute(head, axis, [((i + 1) % count, i) for i in range(ends)]),
            ],
            axis=dim,
        )
    return cells


def from_behind(block, axis, distance):
    devices = range(lax.axis_size(axis))
    route = [(i - distance, i) for i in devices if i - distance in devices]
    return lax.ppermute(block, axis, route)


def attend_kernel(ids, first, last, *refs):
    code_ref, q_ref = refs[0], refs[1]
    count = sum(n for _, n in ids)
    rest = refs[2 + count :]
    stale = []
    at = 2
    for which, n in ids:
        stale.append((which, refs[at], refs[at + n - 1], n == 1))
        at += n
    if not first:
        acc_in, top_in, sum_in = rest[:3]
        rest = rest[3:]
    if last:
        out_ref, acc, top, total = rest
    else:
        acc, top, total = rest
    planes, cols = q_ref.shape[0], q_ref.shape[1]
    tokens = planes * cols
    width = HEADS * HD
    tile = pl.program_id(0)
    scale = HD**-0.5 * LOG2E

    def add_tile(key_of, value_of, fresh):
        def scores(head):
            query = q_ref[:, :, head * HD : (head + 1) * HD].reshape(tokens, HD)
            return lax.dot_general(
                key_of(head), query, (((1,), (1,)), ((), ())), preferred_element_type=jnp.float32
            )

        ready = [scores(head) for head in range(AHEAD)]
        for head in range(HEADS):
            if head + AHEAD < HEADS:
                ready.append(scores(head + AHEAD))
            s = ready[head]
            new = jnp.max(s, axis=0, keepdims=True)
            if not fresh:
                old = top[0, head : head + 1]
                new = jnp.maximum(old, new)
                alpha = jnp.exp2((old - new) * scale)
            p = jnp.exp2((s - new) * scale)
            gain = jnp.sum(p, axis=0, keepdims=True)
            got = lax.dot_general(
                value_of(head),
                p.astype(jnp.bfloat16),
                (((0,), (0,)), ((), ())),
                preferred_element_type=jnp.float32,
            )
            if not fresh:
                gain = total[0, head : head + 1] * alpha + gain
                got = acc[0, head] * alpha + got
            top[0, head : head + 1] = new
            total[0, head : head + 1] = gain
            acc[0, head] = got

    if first:

        def fresh_part(low):
            return q_ref[:, :, low : low + HD].reshape(tokens, HD)

        add_tile(
            lambda head: fresh_part(width + head * HD),
            lambda head: fresh_part(2 * width + head * HD),
            True,
        )
    else:
        acc[...] = acc_in[...]
        top[...] = top_in[...]
        total[...] = sum_in[...]

    def slot(place, carry):
        code = code_ref[tile * 8 + place]
        for which, key_ref, value_ref, joined in stale:

            @pl.when(code >> 2 == which)
            def _():
                here = pl.ds(pl.multiple_of((code & 3) * cols, cols), cols)
                shift = width if joined else 0

                def key_of(head):
                    low = head * HD
                    return key_ref[:, here, low : low + HD].reshape(tokens, HD)

                def value_of(head):
                    low = shift + head * HD
                    return value_ref[:, here, low : low + HD].reshape(tokens, HD)

                add_tile(key_of, value_of, False)

        return carry

    lax.fori_loop(0, 8, slot, 0)
    if last:
        for head in range(HEADS):
            res = acc[0, head] / total[0, head : head + 1]
            res = jnp.transpose(res).astype(jnp.bfloat16)
            out_ref[:, :, head * HD : (head + 1) * HD] = res.reshape(planes, cols, HD)


def attend(code, qkv, sources, state, last, cost):
    ids = tuple((which, len(blocks)) for which, blocks in sources)
    blocks = [block for _, parts in sources for block in parts]
    planes, width, full = qkv.shape
    tiles = code.shape[0] // 8
    cols = width // tiles
    tokens = planes * cols
    first = state is None
    keep = pl.BlockSpec((1, HEADS, HD, tokens), lambda t: (t, 0, 0, 0))
    keep_row = pl.BlockSpec((1, HEADS, tokens), lambda t: (t, 0, 0))

    def whole(block):
        once = pl.Buffered(1)
        return pl.BlockSpec(block.shape, lambda t: (0, 0, 0), pipeline_mode=once)

    part = (planes, cols, HEADS * HD)
    qpart = (planes, cols, full) if first else part
    in_specs = [pl.BlockSpec(memory_space=pltpu.SMEM), pl.BlockSpec(qpart, lambda t: (0, t, 0))]
    in_specs += [whole(block) for block in blocks]
    operands = [code, qkv] + blocks
    if not first:
        in_specs += [keep, keep_row, keep_row]
        operands += list(state)
    kept = jax.ShapeDtypeStruct((tiles, HEADS, HD, tokens), jnp.float32)
    kept_row = jax.ShapeDtypeStruct((tiles, HEADS, tokens), jnp.float32)
    if last:
        out_shape = jax.ShapeDtypeStruct((planes, width, HEADS * HD), jnp.bfloat16)
        out_specs = pl.BlockSpec(part, lambda t: (0, t, 0))
        scratch = [pltpu.VMEM((1, HEADS, HD, tokens), jnp.float32)]
        scratch += [pltpu.VMEM((1, HEADS, tokens), jnp.float32)] * 2
    else:
        out_shape = [kept, kept_row, kept_row]
        out_specs = [keep, keep_row, keep_row]
        scratch = []
    return pl.pallas_call(
        functools.partial(attend_kernel, ids, first, last),
        grid=(tiles,),
        in_specs=in_specs,
        out_specs=out_specs,
        out_shape=out_shape,
        scratch_shapes=scratch,
        compiler_params=pltpu.CompilerParams(vmem_limit_bytes=56 << 20),
        cost_estimate=pl.CostEstimate(
            flops=cost * 1_000_000_000, bytes_accessed=cost * 3_000_000, transcendentals=0
        ),
    )(*operands)


def body(
    hidden,
    control,
    conv_weight,
    ctrl_proj,
    mod_gain,
    mod_shift,
    w_qkv,
    kv_stale,
    key_tiles,
    key_count,
):
    frames, rows, width, dmodel = hidden.shape
    tiles_dev = key_count.shape[2]
    cin = conv_weight.shape[0] // 27
    attn_width = HEADS * HD
    planes = frames * rows
    rim = with_halo(control, (("tm", 0),), 1)
    rim, kv_stale = lax.optimization_barrier((rim, kv_stale))
    below, above = ring_sides(kv_stale)
    rim = with_halo(rim, (("height", 1),), 1)
    rim, kv_late = lax.optimization_barrier((rim, kv_stale))
    rows_before, rows_after, mate = nearest(kv_late)
    grid = rim.reshape(frames + 2, rows + 2, width, cin)
    grid = jnp.pad(grid, ((0, 0), (0, 0), (1, 1), (0, 0)))
    taps = [
        grid[i : i + frames, j : j + rows, k : k + width]
        for i in range(3)
        for j in range(3)
        for k in range(3)
    ]
    stacked = jnp.concatenate(taps, axis=-1).reshape(frames * rows * width, 27 * cin)
    conv = jnp.dot(stacked, conv_weight, preferred_element_type=jnp.float32)
    act = jax.nn.silu(conv).astype(jnp.bfloat16)
    mixed = hidden.reshape(frames * rows * width, dmodel).astype(jnp.float32) + jnp.dot(
        act, ctrl_proj, preferred_element_type=jnp.float32
    )
    center = mixed - jnp.mean(mixed, axis=-1, keepdims=True)
    spread = jnp.mean(center * center, axis=-1, keepdims=True)
    normed = (center * lax.rsqrt(spread + 1e-06) * mod_gain + mod_shift).astype(jnp.bfloat16)
    qkv = jnp.dot(normed, w_qkv, preferred_element_type=jnp.float32).astype(jnp.bfloat16)
    qkv_grid = qkv.reshape(frames, rows, width, 3 * attn_width)
    fresh_kv = qkv_grid[..., attn_width:]
    frame_idx = lax.axis_index("tm")
    row_idx = lax.axis_index("height")
    row_total = lax.axis_size("height")
    idents = key_tiles[0, 0]
    counts = key_count[0, 0]
    dframe = idents // (row_total * tiles_dev) - frame_idx
    drow = idents // tiles_dev % row_total - row_idx
    source = locate(dframe, drow, frame_idx)
    used = lax.broadcasted_iota(jnp.int32, idents.shape, 1) < counts[:, None]
    code = jnp.where(used, source * 4 + idents % tiles_dev, -1).reshape(-1)
    qkv = qkv.reshape(planes, width, 3 * attn_width)

    def add(state, cost, *sources, last=False):
        flat = [
            (which, tuple(part.reshape(planes, width, part.shape[-1]) for part in parts))
            for which, *parts in sources
        ]
        return attend(code, qkv, flat, state, last, cost)

    state = add(None, 20, (0, kv_stale), (3, mate))
    below, above, state = lax.optimization_barrier((below, above, state))
    far_keys, far_values, cross_keys, cross_values, beside = second(below, above, frame_idx)
    near = [(1, rows_before), (2, rows_after), (4, below), (5, above)]
    state = add(state, 30, *near, (6, beside))
    cross_keys, state = lax.optimization_barrier((cross_keys, state))
    trade_keys, mate_keys = third(cross_keys)
    state = add(state, 15, (7, far_keys, far_values))
    cross_values, trade_keys, mate_keys, state = lax.optimization_barrier(
        (cross_values, trade_keys, mate_keys, state)
    )
    trade_values, mate_values = third(cross_values)
    state = add(state, 12, (8, cross_keys, cross_values), (9, mate_keys, mate_values))
    state = add(state, 8, (10, trade_keys, trade_values), last=True)
    return (state.reshape(frames, rows, width, attn_width), fresh_kv)


def solution(mesh):
    placed = (
        P("tm", "height", None, None),
        P("tm", "height", None),
        P(),
        P(),
        P(),
        P(),
        P(),
        P("tm", "height", None, None),
        P("tm", "height", None, None),
        P("tm", "height", None),
    )
    return jax.shard_map(
        body,
        mesh=mesh,
        in_specs=placed,
        out_specs=(P("tm", "height", None, None), P("tm", "height", None, None)),
        check_vma=False,
    )
```
